32 devices in a mesh: tm: 4 (over z), space: 8 (over y, x, core).
Axes of the slice: x: 2, y: 2, z: 4, core: 2. Of those that a mesh axis runs over, the one named last changes fastest.
Arguments:
- tokens: bfloat16 [8192, 1024], P(('tm', 'space')), may hold values from -6 to 6
- latents: bfloat16 [512, 1024], replicated, may hold values from -300 to 300
- up_weight: bfloat16 [1024, 4096], P(None, 'tm'), may hold values from -0.1875 to 0.1875
- down_weight: bfloat16 [4096, 1024], P('tm'), may hold values from -0.09375 to 0.09375
Outputs:
- new_tokens: bfloat16 [8192, 1024], P(('tm', 'space'))
- new_latents: bfloat16 [512, 1024], P('space')
The draws below stay inside these ranges and needn't reach their ends.
All inputs are finite; a program needn't handle non-finite values.
Results may differ from the reference program's by a relative error of at most 0.012.
The reference program's roundings to bfloat16 on the way count: a program that leaves them out, or rounds other values in their place, can miss the bound.
Values may be sent and summed in bfloat16 or wider, within the bound.
A program may use at most 64 MiB of HBM per device.

```python
import jax
import jax.numpy as jnp
from jax import lax

D = 1024
H = 16
FF = 4096
NL = 512
TOK_DEV = 256
TOKENS = 8192


def draw_latents(key, part):
    base = jnp.clip(jax.random.normal(jax.random.fold_in(key, 11), (NL, D), jnp.float32), -5.0, 5.0)
    values = base * 6.0
    return values.astype(jnp.bfloat16)


def block_levels(key, extent, pieces, smallest, top_value):
    def one(dim, shards_of):
        draws = jax.random.uniform(jax.random.fold_in(jax.random.fold_in(key, 6), dim), (shards_of,), jnp.float32, smallest / len(pieces), top_value / len(pieces))
        return jnp.repeat(jnp.exp(draws), extent[dim] // shards_of).reshape((-1,) + (1,) * (len(extent) - dim - 1))

    loudness = one(*pieces[0])
    for cut in pieces[1:]:
        loudness = loudness * one(*cut)
    return loudness


def scatter_about(key, extent, width, bound, shards=(), kind=jnp.bfloat16):
    gain = block_levels(key, extent, shards, -0.22, 0.18) if shards else 1.0
    array = jax.random.normal(key, extent, jnp.float32) * width * gain
    return jnp.minimum(jnp.maximum(array, -bound), bound).astype(kind)


def setup_inputs(seed: int = 0) -> dict:
    key_of = jax.random.split(jax.random.key(seed), 5)
    return {
        "tokens": scatter_about(key_of[0], (TOKENS, D), 1.0, 6.0, ((0, 32),)),
        "latents": draw_latents(jax.random.fold_in(key_of[4], 71), 0),
        "up_weight": scatter_about(key_of[2], (D, FF), D ** -0.5, 0.1875, ((1, 4),)),
        "down_weight": scatter_about(key_of[3], (FF, D), FF ** -0.5, 0.09375, ((0, 4),)),
    }


epsilon = 1e-05
head_groups = 4

def layer_norm(values):
    center = values - lax.optimization_barrier(jnp.mean(values, axis=-1, keepdims=True))
    spread = lax.optimization_barrier(jnp.mean(center * center, axis=-1, keepdims=True))
    return center * lax.rsqrt(spread + epsilon)

def wire_round(values):
    rounded = lax.optimization_barrier(values.astype(jnp.bfloat16))
    return rounded.astype(jnp.float32)

def split_heads(matrix, head_count):
    row_count = matrix.shape[0]
    head_size = matrix.shape[1] // head_count
    return matrix.reshape(row_count, head_groups, head_count // head_groups, head_size).transpose(1, 2, 0, 3)

def per_head(weighted, factor):
    row_count = weighted.shape[0]
    return (weighted.reshape(row_count, factor.shape[1], -1) * factor[:, :, None]).reshape(row_count, weighted.shape[1])

def read_peaks(queries, keys_tok, head_count):
    score_scale = (queries.shape[1] // head_count) ** (-0.5)

    def one_group(operands):
        query_part, key_part = operands
        scores = jnp.einsum('hld,htd->hlt', query_part.astype(jnp.float32), key_part.astype(jnp.float32)) * score_scale
        return lax.optimization_barrier(jnp.max(scores, axis=-1))
    row_peak = lax.map(one_group, (split_heads(queries, head_count), split_heads(keys_tok, head_count)))
    return row_peak.reshape(head_count, queries.shape[0]).T

def read_partial(queries, keys_tok, tokens, head_count):
    score_scale = (queries.shape[1] // head_count) ** (-0.5)

    def one_group(operands):
        query_part, key_part, value_part = operands
        scores = jnp.einsum('hld,htd->hlt', query_part.astype(jnp.float32), key_part.astype(jnp.float32)) * score_scale
        row_peak = lax.optimization_barrier(jnp.max(scores, axis=-1))
        weights = jnp.exp(scores - row_peak[..., None])
        row_total = lax.optimization_barrier(jnp.sum(weights, axis=-1))
        rounded = wire_round(weights)
        weighted = jnp.einsum('hlt,htd->lhd', rounded, value_part.astype(jnp.float32))
        return (row_peak, row_total, weighted)
    row_peak, row_total, weighted = lax.map(one_group, (split_heads(queries, head_count), split_heads(keys_tok, head_count), split_heads(tokens, head_count)))
    latent_count = queries.shape[0]
    row_peak = row_peak.reshape(head_count, latent_count).T
    row_total = row_total.reshape(head_count, latent_count).T
    weighted = weighted.transpose(1, 0, 2, 3).reshape(latent_count, queries.shape[1])
    return (row_peak, row_total, weighted)

def write_tokens(keys_tok, all_latents, tokens, head_count):
    score_scale = (all_latents.shape[1] // head_count) ** (-0.5)
    write_values = layer_norm(all_latents.astype(jnp.float32)).astype(jnp.bfloat16)

    def one_group(operands):
        query_part, key_part, value_part = operands
        scores = jnp.einsum('htd,hld->htl', query_part.astype(jnp.float32), key_part.astype(jnp.float32)) * score_scale
        weights = jnp.exp(scores - lax.optimization_barrier(jnp.max(scores, axis=-1, keepdims=True)))
        shares = (weights / lax.optimization_barrier(jnp.sum(weights, axis=-1, keepdims=True))).astype(jnp.bfloat16)
        return jnp.einsum('htl,hld->thd', shares.astype(jnp.float32), value_part.astype(jnp.float32))
    attended = lax.map(one_group, (split_heads(keys_tok, head_count), split_heads(all_latents, head_count), split_heads(write_values, head_count)))
    token_count = tokens.shape[0]
    attended = attended.transpose(1, 0, 2, 3).reshape(token_count, tokens.shape[1])
    return (tokens.astype(jnp.float32) + attended).astype(jnp.bfloat16)

def reference(tokens, latents, up_weight, down_weight):
    keys_tok = layer_norm(tokens.astype(jnp.float32)).astype(jnp.bfloat16)
    block_count = TOKENS // TOK_DEV
    key_blocks = keys_tok.reshape(block_count, TOK_DEV, D)
    token_blocks = tokens.reshape(block_count, TOK_DEV, D)

    def block_peak_of(key_block):
        return read_peaks(latents, key_block, H)
    block_peaks = lax.map(block_peak_of, key_blocks)
    read_peak = lax.optimization_barrier(jnp.max(block_peaks, axis=0))

    def absorb(carry, operands):
        total_sum, weighted_sum = carry
        block_peak, row_total, weighted = read_partial(latents, operands[0], operands[1], H)
        factor = jnp.exp(block_peak - read_peak)
        total_sum = total_sum + wire_round(row_total * factor)
        weighted_sum = weighted_sum + wire_round(per_head(weighted, factor))
        return ((total_sum, weighted_sum), None)
    initial = (jnp.zeros((NL, H), jnp.float32), jnp.zeros((NL, D), jnp.float32))
    (row_total, weighted), _ = lax.scan(absorb, initial, (key_blocks, token_blocks))
    read_out = (weighted.reshape(NL, H, -1) / row_total[:, :, None]).reshape(NL, D)
    middle = latents.astype(jnp.float32) + read_out
    normed = layer_norm(middle).astype(jnp.bfloat16)
    hidden = jax.nn.gelu(jnp.dot(normed, up_weight, preferred_element_type=jnp.float32), approximate=False).astype(jnp.bfloat16)
    new_latents = (middle + jnp.dot(hidden, down_weight, preferred_element_type=jnp.float32)).astype(jnp.bfloat16)

    def write_block(operands):
        return write_tokens(operands[0], new_latents, operands[1], H)
    new_tokens = lax.map(write_block, (key_blocks, token_blocks)).reshape(TOKENS, D)
    return (new_tokens, new_latents)
```

```python
import functools

import jax
import jax.numpy as jnp
from jax import lax
from jax.experimental import pallas as pl
from jax.experimental.pallas import tpu as pltpu
from jax.sharding import PartitionSpec as P

H = 16
EPSILON = 1e-05
LANES = 128
MESH = pl.DeviceIdType.MESH
F32 = jnp.float32
BF16 = jnp.bfloat16


def layer_norm(values):
    center = values - jnp.mean(values, axis=-1, keepdims=True)
    spread = jnp.mean(center * center, axis=-1, keepdims=True)
    return center * lax.rsqrt(spread + EPSILON)


def dot_nt(left, right):
    return lax.dot_general(
        left, right, (((1,), (1,)), ((), ())), preferred_element_type=F32
    )


def low_half(rows):
    return lax.broadcasted_iota(jnp.int32, (rows, LANES), 1) < LANES // 2


def head_parts(pair, fill):
    values = pair.astype(F32)
    low = low_half(pair.shape[0])
    return (
        jnp.where(low, values, fill).astype(BF16),
        jnp.where(low, fill, values).astype(BF16),
    )


def attend(queries, key_parts, value_parts):
    results, peaks = [], []
    for keys, values in zip(key_parts, value_parts):
        scores = dot_nt(queries, keys)
        peak = jnp.max(scores, axis=-1, keepdims=True)
        weights = jnp.exp(scores - peak).astype(BF16)
        results.append(jnp.dot(weights, values, preferred_element_type=F32))
        peaks.append(peak)
    low = low_half(queries.shape[0])
    weighted = jnp.where(low, results[0], results[1])
    total = pltpu.roll(jnp.where(low, results[1], results[0]), LANES // 2, 1)
    return weighted / total, jnp.where(low, peaks[0], peaks[1]), total


def pair_expansion(width):
    lane = lax.broadcasted_iota(jnp.int32, (LANES, width), 0)
    feature = lax.broadcasted_iota(jnp.int32, (LANES, width), 1)
    half = LANES // 2
    wanted = (feature % LANES) // half * half + feature // LANES
    return jnp.where(lane == wanted, 1.0, 0.0).astype(BF16)


def merge_shares(logs):
    sources, rows, _ = logs.shape
    peak = jnp.max(logs, axis=0)
    weights = jnp.exp(logs - peak[None])
    total = jnp.sum(weights, axis=0)
    shares = (weights / total[None]).reshape(sources * rows, LANES)
    high = shares.astype(BF16)
    low = (shares - high.astype(F32)).astype(BF16)
    return high, low, peak + jnp.log(total)


def kernel(
    n_tm, n_space, pieces,
    tokens_ref, latents_ref, up_hbm, down_hbm, new_tokens_ref, new_latents_ref,
    up_ref, down_ref, keys_ref, send_u, recv_u, send_l, recv_l, merged,
    z_send_u, z_recv_u, z_send_l, z_recv_l, read_out, mlp_send, mlp_recv,
    all_latents, write_values,
    weight_sem, su_send, su_recv, sl_send, sl_recv, zu_send, zu_recv, zl_send, zl_recv,
    ro_send, ro_recv, mlp_ssem, mlp_rsem, gz_send, gz_recv, gs_send, gs_recv,
):
    my_tm = lax.axis_index("tm")
    my_space = lax.axis_index("space")
    width = tokens_ref.shape[1]
    latent_count = latents_ref.shape[0]
    pairs = width // LANES
    rows = latent_count // n_space
    piece_rows = rows // pieces
    scale = (width // H) ** (-0.5)

    def around(count, mine):
        return [lax.rem(mine + k, count) for k in range(1, count)]

    space_peers = around(n_space, my_space)
    tm_peers = around(n_tm, my_tm)

    def copy(src, dst, send_sem, recv_sem, axis, peer):
        return pltpu.make_async_remote_copy(
            src_ref=src, dst_ref=dst, send_sem=send_sem, recv_sem=recv_sem,
            device_id={axis: peer}, device_id_type=MESH,
        )

    barrier = pltpu.get_barrier_semaphore()
    for peer in space_peers:
        pl.semaphore_signal(barrier, inc=1, device_id={"space": peer}, device_id_type=MESH)
    for peer in tm_peers:
        pl.semaphore_signal(barrier, inc=1, device_id={"tm": peer}, device_id_type=MESH)
    up_copy = pltpu.make_async_copy(up_hbm, up_ref, weight_sem.at[0])
    down_copy = pltpu.make_async_copy(down_hbm, down_ref, weight_sem.at[1])
    up_copy.start()
    down_copy.start()

    keys_ref[...] = (
        layer_norm(tokens_ref[...].astype(F32)).astype(BF16).astype(F32) * scale
    ).astype(BF16)
    pl.semaphore_wait(barrier, n_space + n_tm - 2)

    pair_lane = lax.broadcasted_iota(jnp.int32, (latent_count, LANES), 1) % (LANES // 2)

    def read_pair(i, logs):
        lanes = pl.ds(pl.multiple_of(i * LANES, LANES), LANES)
        share, peak, total = attend(
            latents_ref[:, lanes],
            head_parts(keys_ref[:, lanes], 0.0),
            head_parts(tokens_ref[:, lanes], 1.0),
        )
        send_u[:, i] = share.reshape(n_space, rows, LANES).astype(BF16)
        for peer in space_peers:
            copy(
                send_u.at[peer, i], recv_u.at[my_space, i],
                su_send.at[peer], su_recv.at[my_space], "space", peer,
            ).start()
        return jnp.where(pair_lane == i, peak + jnp.log(total), logs)

    logs = lax.fori_loop(0, pairs, read_pair, jnp.zeros((latent_count, LANES), F32))
    send_l[...] = logs.reshape(n_space, rows, LANES)
    for peer in space_peers:
        copy(
            send_l.at[peer], recv_l.at[my_space],
            sl_send.at[peer], sl_recv.at[my_space], "space", peer,
        ).start()
    recv_u[my_space] = send_u[my_space]
    recv_l[my_space] = send_l[my_space]
    expansion = pair_expansion(width)
    for peer in space_peers:
        copy(send_l.at[peer], recv_l.at[peer], sl_send.at[peer], sl_recv.at[peer], "space", peer).wait()
    high, low, merged_log = merge_shares(recv_l[...])
    for peer in space_peers:
        copy(send_u.at[peer], recv_u.at[peer], su_send.at[peer], su_recv.at[peer], "space", peer).wait()
    for i in range(pairs):
        lanes = slice(i * LANES, (i + 1) * LANES)
        factor = jnp.dot(high, expansion[:, lanes], preferred_element_type=F32)
        factor += jnp.dot(low, expansion[:, lanes], preferred_element_type=F32)
        merged[:, lanes] = jnp.sum(
            factor.reshape(n_space, rows, LANES) * recv_u[:, i].astype(F32), axis=0
        )

    mine = my_tm if pieces > 1 else 0
    if pieces > 1:
        z_send_u[...] = merged[...].reshape(pieces, piece_rows, width).astype(BF16)
        z_send_l[...] = merged_log.reshape(pieces, piece_rows, LANES)
    else:
        z_send_u[0] = merged[...].astype(BF16)
        z_send_l[0] = merged_log

    def slot(peer):
        return peer if pieces > 1 else 0

    for peer in tm_peers:
        copy(
            z_send_l.at[slot(peer)], z_recv_l.at[my_tm],
            zl_send.at[peer], zl_recv.at[my_tm], "tm", peer,
        ).start()
        copy(
            z_send_u.at[slot(peer)], z_recv_u.at[my_tm],
            zu_send.at[peer], zu_recv.at[my_tm], "tm", peer,
        ).start()
    z_recv_u[my_tm] = z_send_u[mine]
    z_recv_l[my_tm] = z_send_l[mine]
    for peer in tm_peers:
        copy(z_send_l.at[slot(peer)], z_recv_l.at[peer], zl_send.at[peer], zl_recv.at[peer], "tm", peer).wait()
        copy(z_send_u.at[slot(peer)], z_recv_u.at[peer], zu_send.at[peer], zu_recv.at[peer], "tm", peer).wait()
    high, low, _ = merge_shares(z_recv_l[...])
    factor = jnp.dot(high, expansion, preferred_element_type=F32)
    factor += jnp.dot(low, expansion, preferred_element_type=F32)
    piece = jnp.sum(
        factor.reshape(n_tm, piece_rows, width) * z_recv_u[...].astype(F32), axis=0
    )
    read_out[mine] = piece.astype(BF16)
    if pieces > 1:
        for peer in tm_peers:
            copy(
                read_out.at[my_tm], read_out.at[my_tm],
                ro_send.at[peer], ro_recv.at[my_tm], "tm", peer,
            ).start()
        for peer in tm_peers:
            copy(read_out.at[my_tm], read_out.at[peer], ro_send.at[peer], ro_recv.at[peer], "tm", peer).wait()

    own = pl.ds(pl.multiple_of(my_space * rows, rows), rows)
    merged[...] = latents_ref[own, :].astype(F32) + read_out[...].astype(F32).reshape(rows, width)
    normed = layer_norm(merged[...]).astype(BF16)
    up_copy.wait()
    hidden = jnp.dot(normed, up_ref[...], preferred_element_type=F32)
    hidden = (0.5 * hidden * (1.0 + lax.erf(hidden * (0.5 ** 0.5)))).astype(BF16)
    down_copy.wait()
    terms = jnp.dot(hidden, down_ref[...], preferred_element_type=F32)
    mlp_send[...] = terms.reshape(pieces, piece_rows, width).astype(BF16)
    for peer in tm_peers:
        copy(
            mlp_send.at[slot(peer)], mlp_recv.at[my_tm],
            mlp_ssem.at[peer], mlp_rsem.at[my_tm], "tm", peer,
        ).start()
    mlp_recv[my_tm] = mlp_send[mine]
    own_piece = pl.ds(pl.multiple_of(mine * piece_rows, piece_rows), piece_rows)
    for peer in tm_peers:
        copy(mlp_send.at[slot(peer)], mlp_recv.at[peer], mlp_ssem.at[peer], mlp_rsem.at[peer], "tm", peer).wait()
    all_latents[my_space, mine] = (
        merged[own_piece, :] + jnp.sum(mlp_recv[...].astype(F32), axis=0)
    ).astype(BF16)

    def spread(part):
        for peer in space_peers:
            copy(
                all_latents.at[my_space, part], all_latents.at[my_space, part],
                gs_send.at[peer, part], gs_recv.at[my_space, part], "space", peer,
            ).start()

    if pieces > 1:
        for peer in tm_peers:
            copy(
                all_latents.at[my_space, my_tm], all_latents.at[my_space, my_tm],
                gz_send.at[peer], gz_recv.at[my_tm], "tm", peer,
            ).start()
    spread(mine)
    if pieces > 1:
        for peer in tm_peers:
            copy(
                all_latents.at[my_space, my_tm], all_latents.at[my_space, peer],
                gz_send.at[peer], gz_recv.at[peer], "tm", peer,
            ).wait()
            spread(peer)
    new_latents_ref[...] = (
        all_latents[my_space].astype(F32).reshape(rows, width).astype(BF16)
    )
    for peer in space_peers:
        for part in range(pieces):
            copy(
                all_latents.at[my_space, part], all_latents.at[peer, part],
                gs_send.at[peer, part], gs_recv.at[peer, part], "space", peer,
            ).wait()

    def norm_block(s, carry):
        block = all_latents[s].astype(F32).reshape(rows, width)
        write_values[s] = layer_norm(block).astype(BF16)
        return carry

    lax.fori_loop(0, n_space, norm_block, 0)

    def write_pair(i, carry):
        lanes = pl.ds(pl.multiple_of(i * LANES, LANES), LANES)
        latent_pair = all_latents[:, :, :, lanes].astype(F32).reshape(latent_count, LANES)
        value_pair = write_values[:, :, lanes].astype(F32).reshape(latent_count, LANES)
        low = low_half(latent_count)
        key_parts = (
            jnp.where(low, latent_pair, 0.0).astype(BF16),
            jnp.where(low, 0.0, latent_pair).astype(BF16),
        )
        value_parts = (
            jnp.where(low, value_pair, 1.0).astype(BF16),
            jnp.where(low, 1.0, value_pair).astype(BF16),
        )
        share, _, _ = attend(keys_ref[:, lanes], key_parts, value_parts)
        new_tokens_ref[:, lanes] = (tokens_ref[:, lanes].astype(F32) + share).astype(BF16)
        return carry

    lax.fori_loop(0, pairs, write_pair, 0)


def on_device(n_tm, n_space, tokens, latents, up_weight, down_weight):
    token_count, width = tokens.shape
    latent_count = latents.shape[0]
    rows = latent_count // n_space
    pieces = n_tm if rows % (16 * n_tm) == 0 else 1
    piece_rows = rows // pieces
    pairs = width // LANES
    vmem = pl.BlockSpec(memory_space=pltpu.VMEM)
    anywhere = pl.BlockSpec(memory_space=pl.ANY)
    dma = pltpu.SemaphoreType.DMA
    scratch = [
        pltpu.VMEM(up_weight.shape, BF16),
        pltpu.VMEM(down_weight.shape, BF16),
        pltpu.VMEM((token_count, width), BF16),
        pltpu.VMEM((n_space, pairs, rows, LANES), BF16),
        pltpu.VMEM((n_space, pairs, rows, LANES), BF16),
        pltpu.VMEM((n_space, rows, LANES), F32),
        pltpu.VMEM((n_space, rows, LANES), F32),
        pltpu.VMEM((rows, width), F32),
        pltpu.VMEM((pieces, piece_rows, width), BF16),
        pltpu.VMEM((n_tm, piece_rows, width), BF16),
        pltpu.VMEM((pieces, piece_rows, LANES), F32),
        pltpu.VMEM((n_tm, piece_rows, LANES), F32),
        pltpu.VMEM((pieces, piece_rows, width), BF16),
        pltpu.VMEM((pieces, piece_rows, width), BF16),
        pltpu.VMEM((n_tm, piece_rows, width), BF16),
        pltpu.VMEM((n_space, pieces, piece_rows, width), BF16),
        pltpu.VMEM((n_space, rows, width), BF16),
        dma((2,)),
        dma((n_space,)), dma((n_space,)), dma((n_space,)), dma((n_space,)),
        dma((n_tm,)), dma((n_tm,)), dma((n_tm,)), dma((n_tm,)),
        dma((n_tm,)), dma((n_tm,)), dma((n_tm,)), dma((n_tm,)),
        dma((n_tm,)), dma((n_tm,)),
        dma((n_space, pieces)), dma((n_space, pieces)),
    ]
    return pl.pallas_call(
        functools.partial(kernel, n_tm, n_space, pieces),
        out_shape=(
            jax.ShapeDtypeStruct((token_count, width), BF16),
            jax.ShapeDtypeStruct((rows, width), BF16),
        ),
        in_specs=[vmem, vmem, anywhere, anywhere],
        out_specs=(vmem, vmem),
        scratch_shapes=scratch,
        compiler_params=pltpu.CompilerParams(
            collective_id=0, has_side_effects=True, vmem_limit_bytes=56 * 1024 * 1024
        ),
    )(tokens, latents, up_weight, down_weight)


def solution(mesh):
    n_tm, n_space = mesh.shape["tm"], mesh.shape["space"]
    in_specs = (P(("tm", "space"), None), P(), P(None, "tm"), P("tm", None))
    out_specs = (P(("tm", "space"), None), P("space", None))
    return jax.shard_map(
        functools.partial(on_device, n_tm, n_space),
        mesh=mesh, in_specs=in_specs, out_specs=out_specs, check_vma=False,
    )
```

```python
import functools

import jax
import jax.numpy as jnp
from jax import lax
from jax.experimental import pallas as pl
from jax.experimental.pallas import tpu as pltpu
from jax.sharding import PartitionSpec as P

H = 16
EPSILON = 1e-05
LANES = 128
MESH = pl.DeviceIdType.MESH
F32 = jnp.float32
BF16 = jnp.bfloat16


def layer_norm(values):
    center = values - jnp.mean(values, axis=-1, keepdims=True)
    spread = jnp.mean(center * center, axis=-1, keepdims=True)
    return center * lax.rsqrt(spread + EPSILON)


def dot_nt(left, right):
    return lax.dot_general(
        left, right, (((1,), (1,)), ((), ())), preferred_element_type=F32
    )


def low_half(rows):
    return lax.broadcasted_iota(jnp.int32, (rows, LANES), 1) < LANES // 2


def head_parts(pair, fill):
    values = pair.astype(F32)
    low = low_half(pair.shape[0])
    return (
        jnp.where(low, values, fill).astype(BF16),
        jnp.where(low, fill, values).astype(BF16),
    )


def attend(queries, key_parts, value_parts):
    results, peaks = [], []
    for keys, values in zip(key_parts, value_parts):
        scores = dot_nt(queries, keys)
        peak = jnp.max(scores, axis=-1, keepdims=True)
        weights = jnp.exp(scores - peak).astype(BF16)
        results.append(jnp.dot(weights, values, preferred_element_type=F32))
        peaks.append(peak)
    low = low_half(queries.shape[0])
    weighted = jnp.where(low, results[0], results[1])
    total = pltpu.roll(jnp.where(low, results[1], results[0]), LANES // 2, 1)
    return weighted / total, jnp.where(low, peaks[0], peaks[1]), total


def pair_expansion(width):
    lane = lax.broadcasted_iota(jnp.int32, (LANES, width), 0)
    feature = lax.broadcasted_iota(jnp.int32, (LANES, width), 1)
    half = LANES // 2
    wanted = (feature % LANES) // half * half + feature // LANES
    return jnp.where(lane == wanted, 1.0, 0.0).astype(BF16)


def merge_shares(logs):
    sources, rows, _ = logs.shape
    peak = jnp.max(logs, axis=0)
    weights = jnp.exp(logs - peak[None])
    total = jnp.sum(weights, axis=0)
    shares = (weights / total[None]).reshape(sources * rows, LANES)
    high = shares.astype(BF16)
    low = (shares - high.astype(F32)).astype(BF16)
    return high, low, peak + jnp.log(total)


def kernel(
    n_tm, n_space, pieces,
    tokens_ref, latents_ref, up_hbm, down_hbm, new_tokens_ref, new_latents_ref,
    up_ref, down_ref, keys_ref, send_u, recv_u, send_l, recv_l, merged,
    z_send_u, z_recv_u, z_send_l, z_recv_l, read_out, mlp_send, mlp_recv,
    all_latents, write_values,
    weight_sem, su_send, su_recv, sl_send, sl_recv, zu_send, zu_recv, zl_send, zl_recv,
    ro_send, ro_recv, mlp_ssem, mlp_rsem, gz_send, gz_recv, gs_send, gs_recv,
    gn_send,
):
    my_tm = lax.axis_index("tm")
    my_space = lax.axis_index("space")
    width = tokens_ref.shape[1]
    latent_count = latents_ref.shape[0]
    pairs = width // LANES
    rows = latent_count // n_space
    piece_rows = rows // pieces
    scale = (width // H) ** (-0.5)

    def around(count, mine):
        return [lax.rem(mine + k, count) for k in range(1, count)]

    space_peers = around(n_space, my_space)
    tm_peers = around(n_tm, my_tm)
    paired = n_space % 2 == 0
    near_peers = [my_space + 1 - 2 * lax.rem(my_space, 2)] if paired else []
    far_steps = range(2, n_space, 2) if paired else range(1, n_space)
    far_peers = [lax.rem(my_space + step, n_space) for step in far_steps]

    def copy(src, dst, send_sem, recv_sem, axis, peer):
        return pltpu.make_async_remote_copy(
            src_ref=src, dst_ref=dst, send_sem=send_sem, recv_sem=recv_sem,
            device_id={axis: peer}, device_id_type=MESH,
        )

    barrier = pltpu.get_barrier_semaphore()
    for peer in space_peers:
        pl.semaphore_signal(barrier, inc=1, device_id={"space": peer}, device_id_type=MESH)
    for peer in tm_peers:
        pl.semaphore_signal(barrier, inc=1, device_id={"tm": peer}, device_id_type=MESH)
    up_copy = pltpu.make_async_copy(up_hbm, up_ref, weight_sem.at[0])
    down_copy = pltpu.make_async_copy(down_hbm, down_ref, weight_sem.at[1])
    up_copy.start()
    down_copy.start()

    keys_ref[...] = (
        layer_norm(tokens_ref[...].astype(F32)).astype(BF16).astype(F32) * scale
    ).astype(BF16)
    pl.semaphore_wait(barrier, n_space + n_tm - 2)

    pair_lane = lax.broadcasted_iota(jnp.int32, (latent_count, LANES), 1) % (LANES // 2)

    def read_pair(i, logs):
        lanes = pl.ds(pl.multiple_of(i * LANES, LANES), LANES)
        share, peak, total = attend(
            latents_ref[:, lanes],
            head_parts(keys_ref[:, lanes], 0.0),
            head_parts(tokens_ref[:, lanes], 1.0),
        )
        send_u[:, i] = share.reshape(n_space, rows, LANES).astype(BF16)
        for peer in space_peers:
            copy(
                send_u.at[peer, i], recv_u.at[my_space, i],
                su_send.at[peer], su_recv.at[my_space], "space", peer,
            ).start()
        return jnp.where(pair_lane == i, peak + jnp.log(total), logs)

    logs = lax.fori_loop(0, pairs, read_pair, jnp.zeros((latent_count, LANES), F32))
    send_l[...] = logs.reshape(n_space, rows, LANES)
    for peer in space_peers:
        copy(
            send_l.at[peer], recv_l.at[my_space],
            sl_send.at[peer], sl_recv.at[my_space], "space", peer,
        ).start()
    recv_u[my_space] = send_u[my_space]
    recv_l[my_space] = send_l[my_space]
    expansion = pair_expansion(width)
    for peer in space_peers:
        copy(send_l.at[peer], recv_l.at[peer], sl_send.at[peer], sl_recv.at[peer], "space", peer).wait()
    high, low, merged_log = merge_shares(recv_l[...])
    for peer in space_peers:
        copy(send_u.at[peer], recv_u.at[peer], su_send.at[peer], su_recv.at[peer], "space", peer).wait()
    for i in range(pairs):
        lanes = slice(i * LANES, (i + 1) * LANES)
        factor = jnp.dot(high, expansion[:, lanes], preferred_element_type=F32)
        factor += jnp.dot(low, expansion[:, lanes], preferred_element_type=F32)
        merged[:, lanes] = jnp.sum(
            factor.reshape(n_space, rows, LANES) * recv_u[:, i].astype(F32), axis=0
        )

    mine = my_tm if pieces > 1 else 0
    if pieces > 1:
        z_send_u[...] = merged[...].reshape(pieces, piece_rows, width).astype(BF16)
        z_send_l[...] = merged_log.reshape(pieces, piece_rows, LANES)
    else:
        z_send_u[0] = merged[...].astype(BF16)
        z_send_l[0] = merged_log

    def slot(peer):
        return peer if pieces > 1 else 0

    for peer in tm_peers:
        copy(
            z_send_l.at[slot(peer)], z_recv_l.at[my_tm],
            zl_send.at[peer], zl_recv.at[my_tm], "tm", peer,
        ).start()
        copy(
            z_send_u.at[slot(peer)], z_recv_u.at[my_tm],
            zu_send.at[peer], zu_recv.at[my_tm], "tm", peer,
        ).start()
    z_recv_u[my_tm] = z_send_u[mine]
    z_recv_l[my_tm] = z_send_l[mine]
    for peer in tm_peers:
        copy(z_send_l.at[slot(peer)], z_recv_l.at[peer], zl_send.at[peer], zl_recv.at[peer], "tm", peer).wait()
        copy(z_send_u.at[slot(peer)], z_recv_u.at[peer], zu_send.at[peer], zu_recv.at[peer], "tm", peer).wait()
    high, low, _ = merge_shares(z_recv_l[...])
    factor = jnp.dot(high, expansion, preferred_element_type=F32)
    factor += jnp.dot(low, expansion, preferred_element_type=F32)
    piece = jnp.sum(
        factor.reshape(n_tm, piece_rows, width) * z_recv_u[...].astype(F32), axis=0
    )
    read_out[mine] = piece.astype(BF16)
    if pieces > 1:
        for peer in tm_peers:
            copy(
                read_out.at[my_tm], read_out.at[my_tm],
                ro_send.at[peer], ro_recv.at[my_tm], "tm", peer,
            ).start()
        for peer in tm_peers:
            copy(read_out.at[my_tm], read_out.at[peer], ro_send.at[peer], ro_recv.at[peer], "tm", peer).wait()

    own = pl.ds(pl.multiple_of(my_space * rows, rows), rows)
    merged[...] = latents_ref[own, :].astype(F32) + read_out[...].astype(F32).reshape(rows, width)
    normed = layer_norm(merged[...]).astype(BF16)
    up_copy.wait()
    hidden = jnp.dot(normed, up_ref[...], preferred_element_type=F32)
    hidden = (0.5 * hidden * (1.0 + lax.erf(hidden * (0.5 ** 0.5)))).astype(BF16)
    down_copy.wait()
    terms = jnp.dot(hidden, down_ref[...], preferred_element_type=F32)
    mlp_send[...] = terms.reshape(pieces, piece_rows, width).astype(BF16)
    for peer in tm_peers:
        copy(
            mlp_send.at[slot(peer)], mlp_recv.at[my_tm],
            mlp_ssem.at[peer], mlp_rsem.at[my_tm], "tm", peer,
        ).start()
    mlp_recv[my_tm] = mlp_send[mine]
    own_piece = pl.ds(pl.multiple_of(mine * piece_rows, piece_rows), piece_rows)
    for peer in tm_peers:
        copy(mlp_send.at[slot(peer)], mlp_recv.at[peer], mlp_ssem.at[peer], mlp_rsem.at[peer], "tm", peer).wait()
    all_latents[my_space, mine] = (
        merged[own_piece, :] + jnp.sum(mlp_recv[...].astype(F32), axis=0)
    ).astype(BF16)

    def piece_copy(space, part, peer, send_sem, recv_sem, axis="space"):
        block = all_latents.at[space, part]
        return copy(block, block, send_sem, recv_sem, axis, peer)

    def spread(part):
        for peer in far_peers:
            piece_copy(
                my_space, part, peer, gs_send.at[peer, part], gs_recv.at[my_space, part]
            ).start()
        pass_on(my_space, part)

    def pass_on(space, part):
        for peer in near_peers:
            piece_copy(
                space, part, peer, gn_send.at[space, part], gs_recv.at[space, part]
            ).start()

    if pieces > 1:
        for peer in tm_peers:
            piece_copy(
                my_space, my_tm, peer, gz_send.at[peer], gz_recv.at[my_tm], "tm"
            ).start()
    spread(mine)
    parts = [mine]
    if pieces > 1:
        for peer in tm_peers:
            piece_copy(
                my_space, peer, peer, gz_send.at[peer], gz_recv.at[peer], "tm"
            ).wait_recv()
            spread(peer)
            parts.append(peer)
    new_latents_ref[...] = (
        all_latents[my_space].astype(F32).reshape(rows, width).astype(BF16)
    )
    for part in parts:
        for peer in far_peers:
            piece_copy(
                peer, part, peer, gs_send.at[peer, part], gs_recv.at[peer, part]
            ).wait_recv()
            pass_on(peer, part)
    for part in parts:
        for near in near_peers:
            for space in [near] + [lax.rem(near + step, n_space) for step in far_steps]:
                piece_copy(
                    space, part, near, gn_send.at[my_space, part], gs_recv.at[space, part]
                ).wait_recv()
            for space in [my_space] + far_peers:
                piece_copy(
                    space, part, near, gn_send.at[space, part], gs_recv.at[space, part]
                ).wait_send()
        for peer in far_peers:
            piece_copy(
                my_space, part, peer, gs_send.at[peer, part], gs_recv.at[peer, part]
            ).wait_send()
    if pieces > 1:
        for peer in tm_peers:
            piece_copy(
                my_space, my_tm, peer, gz_send.at[peer], gz_recv.at[peer], "tm"
            ).wait_send()

    def norm_block(s, carry):
        block = all_latents[s].astype(F32).reshape(rows, width)
        write_values[s] = layer_norm(block).astype(BF16)
        return carry

    lax.fori_loop(0, n_space, norm_block, 0)

    def write_pair(i, carry):
        lanes = pl.ds(pl.multiple_of(i * LANES, LANES), LANES)
        latent_pair = all_latents[:, :, :, lanes].astype(F32).reshape(latent_count, LANES)
        value_pair = write_values[:, :, lanes].astype(F32).reshape(latent_count, LANES)
        low = low_half(latent_count)
        key_parts = (
            jnp.where(low, latent_pair, 0.0).astype(BF16),
            jnp.where(low, 0.0, latent_pair).astype(BF16),
        )
        value_parts = (
            jnp.where(low, value_pair, 1.0).astype(BF16),
            jnp.where(low, 1.0, value_pair).astype(BF16),
        )
        share, _, _ = attend(keys_ref[:, lanes], key_parts, value_parts)
        new_tokens_ref[:, lanes] = (tokens_ref[:, lanes].astype(F32) + share).astype(BF16)
        return carry

    lax.fori_loop(0, pairs, write_pair, 0)


def on_device(n_tm, n_space, tokens, latents, up_weight, down_weight):
    token_count, width = tokens.shape
    latent_count = latents.shape[0]
    rows = latent_count // n_space
    pieces = n_tm if rows % (16 * n_tm) == 0 else 1
    piece_rows = rows // pieces
    pairs = width // LANES
    vmem = pl.BlockSpec(memory_space=pltpu.VMEM)
    anywhere = pl.BlockSpec(memory_space=pl.ANY)
    dma = pltpu.SemaphoreType.DMA
    scratch = [
        pltpu.VMEM(up_weight.shape, BF16),
        pltpu.VMEM(down_weight.shape, BF16),
        pltpu.VMEM((token_count, width), BF16),
        pltpu.VMEM((n_space, pairs, rows, LANES), BF16),
        pltpu.VMEM((n_space, pairs, rows, LANES), BF16),
        pltpu.VMEM((n_space, rows, LANES), F32),
        pltpu.VMEM((n_space, rows, LANES), F32),
        pltpu.VMEM((rows, width), F32),
        pltpu.VMEM((pieces, piece_rows, width), BF16),
        pltpu.VMEM((n_tm, piece_rows, width), BF16),
        pltpu.VMEM((pieces, piece_rows, LANES), F32),
        pltpu.VMEM((n_tm, piece_rows, LANES), F32),
        pltpu.VMEM((pieces, piece_rows, width), BF16),
        pltpu.VMEM((pieces, piece_rows, width), BF16),
        pltpu.VMEM((n_tm, piece_rows, width), BF16),
        pltpu.VMEM((n_space, pieces, piece_rows, width), BF16),
        pltpu.VMEM((n_space, rows, width), BF16),
        dma((2,)),
        dma((n_space,)), dma((n_space,)), dma((n_space,)), dma((n_space,)),
        dma((n_tm,)), dma((n_tm,)), dma((n_tm,)), dma((n_tm,)),
        dma((n_tm,)), dma((n_tm,)), dma((n_tm,)), dma((n_tm,)),
        dma((n_tm,)), dma((n_tm,)),
        dma((n_space, pieces)), dma((n_space, pieces)), dma((n_space, pieces)),
    ]
    return pl.pallas_call(
        functools.partial(kernel, n_tm, n_space, pieces),
        out_shape=(
            jax.ShapeDtypeStruct((token_count, width), BF16),
            jax.ShapeDtypeStruct((rows, width), BF16),
        ),
        in_specs=[vmem, vmem, anywhere, anywhere],
        out_specs=(vmem, vmem),
        scratch_shapes=scratch,
        compiler_params=pltpu.CompilerParams(
            collective_id=0, has_side_effects=True, vmem_limit_bytes=56 * 1024 * 1024
        ),
    )(tokens, latents, up_weight, down_weight)


def solution(mesh):
    n_tm, n_space = mesh.shape["tm"], mesh.shape["space"]
    in_specs = (P(("tm", "space"), None), P(), P(None, "tm"), P("tm", None))
    out_specs = (P(("tm", "space"), None), P("space", None))
    return jax.shard_map(
        functools.partial(on_device, n_tm, n_space),
        mesh=mesh, in_specs=in_specs, out_specs=out_specs, check_vma=False,
    )
```

```python
import functools

import jax
import jax.numpy as jnp
from jax import lax
from jax.experimental import pallas as pl
from jax.experimental.pallas import tpu as pltpu
from jax.sharding import PartitionSpec as P

H = 16
EPSILON = 1e-05
LANES = 128
MESH = pl.DeviceIdType.MESH
F32 = jnp.float32
BF16 = jnp.bfloat16


def layer_norm(values):
    center = values - jnp.mean(values, axis=-1, keepdims=True)
    spread = jnp.mean(center * center, axis=-1, keepdims=True)
    return center * lax.rsqrt(spread + EPSILON)


def dot_nt(left, right):
    return lax.dot_general(
        left, right, (((1,), (1,)), ((), ())), preferred_element_type=F32
    )


def low_half(rows):
    return lax.broadcasted_iota(jnp.int32, (rows, LANES), 1) < LANES // 2


def head_parts(pair, fill):
    values = pair.astype(F32)
    low = low_half(pair.shape[0])
    return (
        jnp.where(low, values, fill).astype(BF16),
        jnp.where(low, fill, values).astype(BF16),
    )


def attend(queries, key_parts, value_parts):
    results, peaks = [], []
    for keys, values in zip(key_parts, value_parts):
        scores = dot_nt(queries, keys)
        peak = jnp.max(scores, axis=-1, keepdims=True)
        weights = jnp.exp(scores - peak).astype(BF16)
        results.append(jnp.dot(weights, values, preferred_element_type=F32))
        peaks.append(peak)
    low = low_half(queries.shape[0])
    weighted = jnp.where(low, results[0], results[1])
    total = pltpu.roll(jnp.where(low, results[1], results[0]), LANES // 2, 1)
    return weighted / total, jnp.where(low, peaks[0], peaks[1]), total


def pair_expansion(width):
    lane = lax.broadcasted_iota(jnp.int32, (LANES, width), 0)
    feature = lax.broadcasted_iota(jnp.int32, (LANES, width), 1)
    half = LANES // 2
    wanted = (feature % LANES) // half * half + feature // LANES
    return jnp.where(lane == wanted, 1.0, 0.0).astype(BF16)


def merge_shares(logs):
    sources, rows, _ = logs.shape
    peak = jnp.max(logs, axis=0)
    weights = jnp.exp(logs - peak[None])
    total = jnp.sum(weights, axis=0)
    shares = (weights / total[None]).reshape(sources * rows, LANES)
    high = shares.astype(BF16)
    low = (shares - high.astype(F32)).astype(BF16)
    return high, low, peak + jnp.log(total)


def kernel(
    n_tm, n_space, pieces,
    tokens_ref, latents_ref, up_hbm, down_hbm, new_tokens_ref, new_latents_ref,
    up_ref, down_ref, keys_ref, send_u, recv_u, send_l, recv_l, merged,
    pair_tokens, pair_keys, half_u, half_l, pair_u, pair_l,
    z_send_u, z_recv_u, z_send_l, z_recv_l, read_out, mlp_send, mlp_recv,
    all_latents, write_values,
    weight_sem, su_send, su_recv, sl_send, sl_recv, zu_send, zu_recv, zl_send, zl_recv,
    ro_send, ro_recv, mlp_ssem, mlp_rsem, gz_send, gz_recv, gs_send, gs_recv,
    gn_send, pt_send, pt_recv, sw_send, sw_recv,
):
    my_tm = lax.axis_index("tm")
    my_space = lax.axis_index("space")
    width = tokens_ref.shape[1]
    latent_count = latents_ref.shape[0]
    pairs = width // LANES
    rows = latent_count // n_space
    piece_rows = rows // pieces
    scale = (width // H) ** (-0.5)

    def around(count, mine):
        return [lax.rem(mine + k, count) for k in range(1, count)]

    tm_peers = around(n_tm, my_tm)
    near_peers = [my_space + 1 - 2 * lax.rem(my_space, 2)]
    far_steps = range(2, n_space, 2)
    far_peers = [lax.rem(my_space + step, n_space) for step in far_steps]

    def copy(src, dst, send_sem, recv_sem, axis, peer):
        return pltpu.make_async_remote_copy(
            src_ref=src, dst_ref=dst, send_sem=send_sem, recv_sem=recv_sem,
            device_id={axis: peer}, device_id_type=MESH,
        )

    barrier = pltpu.get_barrier_semaphore()
    for peer in near_peers + far_peers:
        pl.semaphore_signal(barrier, inc=1, device_id={"space": peer}, device_id_type=MESH)
    for peer in tm_peers:
        pl.semaphore_signal(barrier, inc=1, device_id={"tm": peer}, device_id_type=MESH)
    up_copy = pltpu.make_async_copy(up_hbm, up_ref, weight_sem.at[0])
    down_copy = pltpu.make_async_copy(down_hbm, down_ref, weight_sem.at[1])
    up_copy.start()
    down_copy.start()

    pl.semaphore_wait(barrier, len(near_peers) + len(far_peers) + n_tm - 1)

    near = near_peers[0]
    parity = lax.rem(my_space, 2)
    chip = my_space // 2
    token_count = tokens_ref.shape[0]
    half_width = width // 2
    half_pairs = pairs // 2
    own_half = pl.ds(pl.multiple_of(parity * half_width, half_width), half_width)
    near_half = pl.ds(pl.multiple_of((1 - parity) * half_width, half_width), half_width)
    token_copy = copy(
        tokens_ref.at[:, near_half], pair_tokens.at[1], pt_send.at[0], pt_recv.at[0], "space", near
    )
    key_copy = copy(
        keys_ref.at[:, near_half], pair_keys.at[1], pt_send.at[1], pt_recv.at[1], "space", near
    )
    token_copy.start()
    keys_ref[...] = (
        layer_norm(tokens_ref[...].astype(F32)).astype(BF16).astype(F32) * scale
    ).astype(BF16)
    key_copy.start()
    pair_tokens[0] = tokens_ref[:, own_half]
    pair_keys[0] = keys_ref[:, own_half]
    expansion = pair_expansion(width)
    lane = lax.broadcasted_iota(jnp.int32, (latent_count, LANES), 1) % (LANES // 2)
    token_copy.wait()
    key_copy.wait()

    def read_pair(i, logs):
        lanes = pl.ds(pl.multiple_of(i * LANES, LANES), LANES)
        all_lanes = pl.ds(pl.multiple_of(parity * half_width + i * LANES, LANES), LANES)
        share, peak, total = attend(
            latents_ref[:, all_lanes],
            head_parts(pair_keys[:, :, lanes].reshape(2 * token_count, LANES), 0.0),
            head_parts(pair_tokens[:, :, lanes].reshape(2 * token_count, LANES), 1.0),
        )
        send_u[:, i] = share.reshape(n_space // 2, 2 * rows, LANES).astype(BF16)
        for peer in far_peers:
            copy(
                send_u.at[peer // 2, i], recv_u.at[chip, i],
                su_send.at[peer], su_recv.at[my_space], "space", peer,
            ).start()
        return jnp.where(lane == i, peak + jnp.log(total), logs)

    logs = lax.fori_loop(0, half_pairs, read_pair, jnp.zeros((latent_count, LANES), F32))
    first = logs.astype(BF16).astype(F32)
    second = (logs - first).astype(BF16).astype(F32)
    third = logs - first - second
    terms = jnp.where(
        lane < 16, first, jnp.where(lane < 32, pltpu.roll(second, 16, 1), pltpu.roll(third, 32, 1))
    )
    send_l[...] = terms.reshape(n_space // 2, 2 * rows, LANES).astype(BF16)
    for peer in far_peers:
        copy(
            send_l.at[peer // 2], recv_l.at[chip],
            sl_send.at[peer], sl_recv.at[my_space], "space", peer,
        ).start()
    recv_u[chip] = send_u[chip]
    recv_l[chip] = send_l[chip]
    for peer in far_peers:
        copy(send_l.at[peer // 2], recv_l.at[peer // 2], sl_send.at[peer], sl_recv.at[peer], "space", peer).wait()
    terms = recv_l[...].astype(F32).reshape(latent_count, LANES)
    logs = terms + pltpu.roll(terms, LANES - 16, 1) + pltpu.roll(terms, LANES - 32, 1)
    high, low, merged_log = merge_shares(logs.reshape(n_space // 2, 2 * rows, LANES))
    half_l[...] = merged_log.reshape(2, rows, LANES)
    for peer in far_peers:
        copy(send_u.at[peer // 2], recv_u.at[peer // 2], su_send.at[peer], su_recv.at[peer], "space", peer).wait()
    for i in range(half_pairs):
        lanes = slice(i * LANES, (i + 1) * LANES)
        factor = jnp.dot(high, expansion[:, lanes], preferred_element_type=F32)
        factor += jnp.dot(low, expansion[:, lanes], preferred_element_type=F32)
        half_u[:, :, lanes] = jnp.sum(
            factor.reshape(n_space // 2, 2 * rows, LANES) * recv_u[:, i].astype(F32), axis=0
        ).reshape(2, rows, LANES).astype(BF16)

    swap_l = copy(
        half_l.at[1 - parity], pair_l.at[parity], sw_send.at[0], sw_recv.at[0], "space", near
    )
    swap_u = copy(
        half_u.at[1 - parity], pair_u.at[parity], sw_send.at[1], sw_recv.at[1], "space", near
    )
    swap_l.start()
    swap_u.start()
    pair_l[parity] = half_l[parity]
    pair_u[parity] = half_u[parity]
    copy(half_l.at[1 - parity], pair_l.at[1 - parity], sw_send.at[0], sw_recv.at[0], "space", near).wait()
    copy(half_u.at[1 - parity], pair_u.at[1 - parity], sw_send.at[1], sw_recv.at[1], "space", near).wait()
    row_lane = lax.broadcasted_iota(jnp.int32, (rows, LANES), 1) % (LANES // 2)
    merged_log = jnp.where(row_lane < half_pairs, pair_l[0], pltpu.roll(pair_l[1], half_pairs, 1))
    for half in range(2):
        merged[:, half * half_width:(half + 1) * half_width] = pair_u[half].astype(F32)

    mine = my_tm if pieces > 1 else 0
    if pieces > 1:
        z_send_u[...] = merged[...].reshape(pieces, piece_rows, width).astype(BF16)
        z_send_l[...] = merged_log.reshape(pieces, piece_rows, LANES)
    else:
        z_send_u[0] = merged[...].astype(BF16)
        z_send_l[0] = merged_log

    def slot(peer):
        return peer if pieces > 1 else 0

    for peer in tm_peers:
        copy(
            z_send_l.at[slot(peer)], z_recv_l.at[my_tm],
            zl_send.at[peer], zl_recv.at[my_tm], "tm", peer,
        ).start()
        copy(
            z_send_u.at[slot(peer)], z_recv_u.at[my_tm],
            zu_send.at[peer], zu_recv.at[my_tm], "tm", peer,
        ).start()
    z_recv_u[my_tm] = z_send_u[mine]
    z_recv_l[my_tm] = z_send_l[mine]
    for peer in tm_peers:
        copy(z_send_l.at[slot(peer)], z_recv_l.at[peer], zl_send.at[peer], zl_recv.at[peer], "tm", peer).wait()
        copy(z_send_u.at[slot(peer)], z_recv_u.at[peer], zu_send.at[peer], zu_recv.at[peer], "tm", peer).wait()
    high, low, _ = merge_shares(z_recv_l[...])
    factor = jnp.dot(high, expansion, preferred_element_type=F32)
    factor += jnp.dot(low, expansion, preferred_element_type=F32)
    piece = jnp.sum(
        factor.reshape(n_tm, piece_rows, width) * z_recv_u[...].astype(F32), axis=0
    )
    read_out[mine] = piece.astype(BF16)
    if pieces > 1:
        for peer in tm_peers:
            copy(
                read_out.at[my_tm], read_out.at[my_tm],
                ro_send.at[peer], ro_recv.at[my_tm], "tm", peer,
            ).start()
        for peer in tm_peers:
            copy(read_out.at[my_tm], read_out.at[peer], ro_send.at[peer], ro_recv.at[peer], "tm", peer).wait()

    own = pl.ds(pl.multiple_of(my_space * rows, rows), rows)
    merged[...] = latents_ref[own, :].astype(F32) + read_out[...].astype(F32).reshape(rows, width)
    normed = layer_norm(merged[...]).astype(BF16)
    up_copy.wait()
    hidden = jnp.dot(normed, up_ref[...], preferred_element_type=F32)
    hidden = (0.5 * hidden * (1.0 + lax.erf(hidden * (0.5 ** 0.5)))).astype(BF16)
    down_copy.wait()
    terms = jnp.dot(hidden, down_ref[...], preferred_element_type=F32)
    mlp_send[...] = terms.reshape(pieces, piece_rows, width).astype(BF16)
    for peer in tm_peers:
        copy(
            mlp_send.at[slot(peer)], mlp_recv.at[my_tm],
            mlp_ssem.at[peer], mlp_rsem.at[my_tm], "tm", peer,
        ).start()
    mlp_recv[my_tm] = mlp_send[mine]
    own_piece = pl.ds(pl.multiple_of(mine * piece_rows, piece_rows), piece_rows)
    for peer in tm_peers:
        copy(mlp_send.at[slot(peer)], mlp_recv.at[peer], mlp_ssem.at[peer], mlp_rsem.at[peer], "tm", peer).wait()
    all_latents[my_space, mine] = (
        merged[own_piece, :] + jnp.sum(mlp_recv[...].astype(F32), axis=0)
    ).astype(BF16)

    def piece_copy(space, part, peer, send_sem, recv_sem, axis="space"):
        block = all_latents.at[space, part]
        return copy(block, block, send_sem, recv_sem, axis, peer)

    def spread(part):
        for peer in far_peers:
            piece_copy(
                my_space, part, peer, gs_send.at[peer, part], gs_recv.at[my_space, part]
            ).start()
        pass_on(my_space, part)

    def pass_on(space, part):
        for peer in near_peers:
            piece_copy(
                space, part, peer, gn_send.at[space, part], gs_recv.at[space, part]
            ).start()

    if pieces > 1:
        for peer in tm_peers:
            piece_copy(
                my_space, my_tm, peer, gz_send.at[peer], gz_recv.at[my_tm], "tm"
            ).start()
    spread(mine)
    parts = [mine]
    if pieces > 1:
        for peer in tm_peers:
            piece_copy(
                my_space, peer, peer, gz_send.at[peer], gz_recv.at[peer], "tm"
            ).wait_recv()
            spread(peer)
            parts.append(peer)
    new_latents_ref[...] = (
        all_latents[my_space].astype(F32).reshape(rows, width).astype(BF16)
    )
    for part in parts:
        for peer in far_peers:
            piece_copy(
                peer, part, peer, gs_send.at[peer, part], gs_recv.at[peer, part]
            ).wait_recv()
            pass_on(peer, part)
    for part in parts:
        for near in near_peers:
            for space in [near] + [lax.rem(near + step, n_space) for step in far_steps]:
                piece_copy(
                    space, part, near, gn_send.at[my_space, part], gs_recv.at[space, part]
                ).wait_recv()
            for space in [my_space] + far_peers:
                piece_copy(
                    space, part, near, gn_send.at[space, part], gs_recv.at[space, part]
                ).wait_send()
        for peer in far_peers:
            piece_copy(
                my_space, part, peer, gs_send.at[peer, part], gs_recv.at[peer, part]
            ).wait_send()
    if pieces > 1:
        for peer in tm_peers:
            piece_copy(
                my_space, my_tm, peer, gz_send.at[peer], gz_recv.at[peer], "tm"
            ).wait_send()

    def norm_block(s, carry):
        block = all_latents[s].astype(F32).reshape(rows, width)
        write_values[s] = layer_norm(block).astype(BF16)
        return carry

    lax.fori_loop(0, n_space, norm_block, 0)

    def write_pair(i, carry):
        lanes = pl.ds(pl.multiple_of(i * LANES, LANES), LANES)
        latent_pair = all_latents[:, :, :, lanes].astype(F32).reshape(latent_count, LANES)
        value_pair = write_values[:, :, lanes].astype(F32).reshape(latent_count, LANES)
        low = low_half(latent_count)
        key_parts = (
            jnp.where(low, latent_pair, 0.0).astype(BF16),
            jnp.where(low, 0.0, latent_pair).astype(BF16),
        )
        value_parts = (
            jnp.where(low, value_pair, 1.0).astype(BF16),
            jnp.where(low, 1.0, value_pair).astype(BF16),
        )
        share, _, _ = attend(keys_ref[:, lanes], key_parts, value_parts)
        new_tokens_ref[:, lanes] = (tokens_ref[:, lanes].astype(F32) + share).astype(BF16)
        return carry

    lax.fori_loop(0, pairs, write_pair, 0)


def on_device(n_tm, n_space, tokens, latents, up_weight, down_weight):
    token_count, width = tokens.shape
    latent_count = latents.shape[0]
    rows = latent_count // n_space
    pieces = n_tm if rows % (16 * n_tm) == 0 else 1
    piece_rows = rows // pieces
    pairs = width // LANES
    vmem = pl.BlockSpec(memory_space=pltpu.VMEM)
    anywhere = pl.BlockSpec(memory_space=pl.ANY)
    dma = pltpu.SemaphoreType.DMA
    scratch = [
        pltpu.VMEM(up_weight.shape, BF16),
        pltpu.VMEM(down_weight.shape, BF16),
        pltpu.VMEM((token_count, width), BF16),
        pltpu.VMEM((n_space // 2, pairs // 2, 2 * rows, LANES), BF16),
        pltpu.VMEM((n_space // 2, pairs // 2, 2 * rows, LANES), BF16),
        pltpu.VMEM((n_space // 2, 2 * rows, LANES), BF16),
        pltpu.VMEM((n_space // 2, 2 * rows, LANES), BF16),
        pltpu.VMEM((rows, width), F32),
        pltpu.VMEM((2, token_count, width // 2), BF16),
        pltpu.VMEM((2, token_count, width // 2), BF16),
        pltpu.VMEM((2, rows, width // 2), BF16),
        pltpu.VMEM((2, rows, LANES), F32),
        pltpu.VMEM((2, rows, width // 2), BF16),
        pltpu.VMEM((2, rows, LANES), F32),
        pltpu.VMEM((pieces, piece_rows, width), BF16),
        pltpu.VMEM((n_tm, piece_rows, width), BF16),
        pltpu.VMEM((pieces, piece_rows, LANES), F32),
        pltpu.VMEM((n_tm, piece_rows, LANES), F32),
        pltpu.VMEM((pieces, piece_rows, width), BF16),
        pltpu.VMEM((pieces, piece_rows, width), BF16),
        pltpu.VMEM((n_tm, piece_rows, width), BF16),
        pltpu.VMEM((n_space, pieces, piece_rows, width), BF16),
        pltpu.VMEM((n_space, rows, width), BF16),
        dma((2,)),
        dma((n_space,)), dma((n_space,)), dma((n_space,)), dma((n_space,)),
        dma((n_tm,)), dma((n_tm,)), dma((n_tm,)), dma((n_tm,)),
        dma((n_tm,)), dma((n_tm,)), dma((n_tm,)), dma((n_tm,)),
        dma((n_tm,)), dma((n_tm,)),
        dma((n_space, pieces)), dma((n_space, pieces)), dma((n_space, pieces)),
        dma((2,)), dma((2,)), dma((2,)), dma((2,)),
    ]
    return pl.pallas_call(
        functools.partial(kernel, n_tm, n_space, pieces),
        out_shape=(
            jax.ShapeDtypeStruct((token_count, width), BF16),
            jax.ShapeDtypeStruct((rows, width), BF16),
        ),
        in_specs=[vmem, vmem, anywhere, anywhere],
        out_specs=(vmem, vmem),
        scratch_shapes=scratch,
        compiler_params=pltpu.CompilerParams(
            collective_id=0, has_side_effects=True, vmem_limit_bytes=56 * 1024 * 1024
        ),
    )(tokens, latents, up_weight, down_weight)


def solution(mesh):
    n_tm, n_space = mesh.shape["tm"], mesh.shape["space"]
    in_specs = (P(("tm", "space"), None), P(), P(None, "tm"), P("tm", None))
    out_specs = (P(("tm", "space"), None), P("space", None))
    return jax.shard_map(
        functools.partial(on_device, n_tm, n_space),
        mesh=mesh, in_specs=in_specs, out_specs=out_specs, check_vma=False,
    )
```

```python
import functools

import jax
import jax.numpy as jnp
from jax import lax
from jax.experimental import pallas as pl
from jax.experimental.pallas import tpu as pltpu
from jax.sharding import PartitionSpec as P

H = 16
EPSILON = 1e-05
LANES = 128
MESH = pl.DeviceIdType.MESH
F32 = jnp.float32
BF16 = jnp.bfloat16


def layer_norm(values):
    center = values - jnp.mean(values, axis=-1, keepdims=True)
    spread = jnp.mean(center * center, axis=-1, keepdims=True)
    return center * lax.rsqrt(spread + EPSILON)


def dot_nt(left, right):
    return lax.dot_general(
        left, right, (((1,), (1,)), ((), ())), preferred_element_type=F32
    )


def low_half(rows):
    return lax.broadcasted_iota(jnp.int32, (rows, LANES), 1) < LANES // 2


def head_parts(pair, fill):
    values = pair.astype(F32)
    low = low_half(pair.shape[0])
    return (
        jnp.where(low, values, fill).astype(BF16),
        jnp.where(low, fill, values).astype(BF16),
    )


def attend(queries, key_parts, value_parts):
    results, peaks = [], []
    for keys, values in zip(key_parts, value_parts):
        scores = dot_nt(queries, keys)
        peak = jnp.max(scores, axis=-1, keepdims=True)
        weights = jnp.exp(scores - peak).astype(BF16)
        results.append(jnp.dot(weights, values, preferred_element_type=F32))
        peaks.append(peak)
    low = low_half(queries.shape[0])
    weighted = jnp.where(low, results[0], results[1])
    total = pltpu.roll(jnp.where(low, results[1], results[0]), LANES // 2, 1)
    return weighted / total, jnp.where(low, peaks[0], peaks[1]), total


def pair_expansion(width):
    lane = lax.broadcasted_iota(jnp.int32, (LANES, width), 0)
    feature = lax.broadcasted_iota(jnp.int32, (LANES, width), 1)
    half = LANES // 2
    wanted = (feature % LANES) // half * half + feature // LANES
    return jnp.where(lane == wanted, 1.0, 0.0).astype(BF16)


def merge_shares(logs):
    sources, rows, _ = logs.shape
    peak = jnp.max(logs, axis=0)
    weights = jnp.exp(logs - peak[None])
    total = jnp.sum(weights, axis=0)
    shares = (weights / total[None]).reshape(sources * rows, LANES)
    high = shares.astype(BF16)
    low = (shares - high.astype(F32)).astype(BF16)
    return high, low, peak + jnp.log(total)


def kernel(
    n_tm, n_space, pieces,
    tokens_ref, latents_ref, up_hbm, down_hbm, new_tokens_ref, new_latents_ref,
    up_ref, down_ref, keys_ref, send_u, recv_u, send_l, recv_l, merged,
    pair_tokens, pair_keys, half_u, half_l, pair_u, pair_l,
    z_send_u, z_recv_u, z_send_l, z_recv_l, read_out, mlp_send, mlp_recv,
    all_latents, write_values,
    weight_sem, su_send, su_recv, sl_send, sl_recv, zu_send, zu_recv, zl_send, zl_recv,
    ro_send, ro_recv, mlp_ssem, mlp_rsem, gz_send, gz_recv, gs_send, gs_recv,
    gn_send, pt_send, pt_recv, sw_send, sw_recv,
):
    my_tm = lax.axis_index("tm")
    my_space = lax.axis_index("space")
    width = tokens_ref.shape[1]
    latent_count = latents_ref.shape[0]
    pairs = width // LANES
    rows = latent_count // n_space
    piece_rows = rows // pieces
    scale = (width // H) ** (-0.5)

    def around(count, mine):
        return [lax.rem(mine + k, count) for k in range(1, count)]

    tm_peers = around(n_tm, my_tm)
    near_peers = [my_space + 1 - 2 * lax.rem(my_space, 2)]
    far_steps = range(2, n_space, 2)
    far_peers = [lax.rem(my_space + step, n_space) for step in far_steps]

    def copy(src, dst, send_sem, recv_sem, axis, peer):
        return pltpu.make_async_remote_copy(
            src_ref=src, dst_ref=dst, send_sem=send_sem, recv_sem=recv_sem,
            device_id={axis: peer}, device_id_type=MESH,
        )

    barrier = pltpu.get_barrier_semaphore()
    for peer in near_peers + far_peers:
        pl.semaphore_signal(barrier, inc=1, device_id={"space": peer}, device_id_type=MESH)
    for peer in tm_peers:
        pl.semaphore_signal(barrier, inc=1, device_id={"tm": peer}, device_id_type=MESH)
    up_copy = pltpu.make_async_copy(up_hbm, up_ref, weight_sem.at[0])
    down_copy = pltpu.make_async_copy(down_hbm, down_ref, weight_sem.at[1])
    up_copy.start()
    down_copy.start()

    pl.semaphore_wait(barrier, len(near_peers) + len(far_peers) + n_tm - 1)

    near = near_peers[0]
    parity = lax.rem(my_space, 2)
    chip = my_space // 2
    token_count = tokens_ref.shape[0]
    half_width = width // 2
    half_pairs = pairs // 2
    own_half = pl.ds(pl.multiple_of(parity * half_width, half_width), half_width)
    near_half = pl.ds(pl.multiple_of((1 - parity) * half_width, half_width), half_width)
    token_copy = copy(
        tokens_ref.at[:, near_half], pair_tokens.at[1], pt_send.at[0], pt_recv.at[0], "space", near
    )
    key_copy = copy(
        keys_ref.at[:, near_half], pair_keys.at[1], pt_send.at[1], pt_recv.at[1], "space", near
    )
    token_copy.start()
    keys_ref[...] = (
        layer_norm(tokens_ref[...].astype(F32)).astype(BF16).astype(F32) * scale
    ).astype(BF16)
    key_copy.start()
    pair_tokens[0] = tokens_ref[:, own_half]
    pair_keys[0] = keys_ref[:, own_half]
    expansion = pair_expansion(width)
    lane = lax.broadcasted_iota(jnp.int32, (latent_count, LANES), 1) % (LANES // 2)
    token_copy.wait()
    key_copy.wait()

    def read_pair(i, logs):
        lanes = pl.ds(pl.multiple_of(i * LANES, LANES), LANES)
        all_lanes = pl.ds(pl.multiple_of(parity * half_width + i * LANES, LANES), LANES)
        share, peak, total = attend(
            latents_ref[:, all_lanes],
            head_parts(pair_keys[:, :, lanes].reshape(2 * token_count, LANES), 0.0),
            head_parts(pair_tokens[:, :, lanes].reshape(2 * token_count, LANES), 1.0),
        )
        send_u[:, i] = share.reshape(n_space // 2, 2 * rows, LANES).astype(BF16)
        for peer in far_peers:
            copy(
                send_u.at[peer // 2, i], recv_u.at[chip, i],
                su_send.at[peer], su_recv.at[my_space], "space", peer,
            ).start()
        return jnp.where(lane == i, peak + jnp.log(total), logs)

    logs = lax.fori_loop(0, half_pairs, read_pair, jnp.zeros((latent_count, LANES), F32))
    first = logs.astype(BF16).astype(F32)
    second = (logs - first).astype(BF16).astype(F32)
    third = logs - first - second
    terms = jnp.where(
        lane < 16, first, jnp.where(lane < 32, pltpu.roll(second, 16, 1), pltpu.roll(third, 32, 1))
    )
    send_l[...] = terms.reshape(n_space // 2, 2 * rows, LANES).astype(BF16)
    for peer in far_peers:
        copy(
            send_l.at[peer // 2], recv_l.at[chip],
            sl_send.at[peer], sl_recv.at[my_space], "space", peer,
        ).start()
    recv_u[chip] = send_u[chip]
    recv_l[chip] = send_l[chip]
    for peer in far_peers:
        copy(send_l.at[peer // 2], recv_l.at[peer // 2], sl_send.at[peer], sl_recv.at[peer], "space", peer).wait()
    terms = recv_l[...].astype(F32).reshape(latent_count, LANES)
    logs = terms + pltpu.roll(terms, LANES - 16, 1) + pltpu.roll(terms, LANES - 32, 1)
    high, low, merged_log = merge_shares(logs.reshape(n_space // 2, 2 * rows, LANES))
    half_l[...] = merged_log.reshape(2, rows, LANES)
    for peer in far_peers:
        copy(send_u.at[peer // 2], recv_u.at[peer // 2], su_send.at[peer], su_recv.at[peer], "space", peer).wait()
    for i in range(half_pairs):
        lanes = slice(i * LANES, (i + 1) * LANES)
        factor = jnp.dot(high, expansion[:, lanes], preferred_element_type=F32)
        factor += jnp.dot(low, expansion[:, lanes], preferred_element_type=F32)
        half_u[:, :, lanes] = jnp.sum(
            factor.reshape(n_space // 2, 2 * rows, LANES) * recv_u[:, i].astype(F32), axis=0
        ).reshape(2, rows, LANES).astype(BF16)

    swap_l = copy(
        half_l.at[1 - parity], pair_l.at[parity], sw_send.at[0], sw_recv.at[0], "space", near
    )
    swap_u = copy(
        half_u.at[1 - parity], pair_u.at[parity], sw_send.at[1], sw_recv.at[1], "space", near
    )
    swap_l.start()
    swap_u.start()
    pair_l[parity] = half_l[parity]
    pair_u[parity] = half_u[parity]
    copy(half_l.at[1 - parity], pair_l.at[1 - parity], sw_send.at[0], sw_recv.at[0], "space", near).wait()
    copy(half_u.at[1 - parity], pair_u.at[1 - parity], sw_send.at[1], sw_recv.at[1], "space", near).wait()
    row_lane = lax.broadcasted_iota(jnp.int32, (rows, LANES), 1) % (LANES // 2)
    merged_log = jnp.where(row_lane < half_pairs, pair_l[0], pltpu.roll(pair_l[1], half_pairs, 1))
    for half in range(2):
        merged[:, half * half_width:(half + 1) * half_width] = pair_u[half].astype(F32)

    mine = my_tm if pieces > 1 else 0
    if pieces > 1:
        z_send_u[...] = merged[...].reshape(pieces, piece_rows, width).astype(BF16)
        z_send_l[...] = merged_log.reshape(pieces, piece_rows, LANES)
    else:
        z_send_u[0] = merged[...].astype(BF16)
        z_send_l[0] = merged_log

    def slot(peer):
        return peer if pieces > 1 else 0

    for peer in tm_peers:
        copy(
            z_send_l.at[slot(peer)], z_recv_l.at[my_tm],
            zl_send.at[peer], zl_recv.at[my_tm], "tm", peer,
        ).start()
        copy(
            z_send_u.at[slot(peer)], z_recv_u.at[my_tm],
            zu_send.at[peer], zu_recv.at[my_tm], "tm", peer,
        ).start()
    z_recv_u[my_tm] = z_send_u[mine]
    z_recv_l[my_tm] = z_send_l[mine]
    for peer in tm_peers:
        copy(z_send_l.at[slot(peer)], z_recv_l.at[peer], zl_send.at[peer], zl_recv.at[peer], "tm", peer).wait()
        copy(z_send_u.at[slot(peer)], z_recv_u.at[peer], zu_send.at[peer], zu_recv.at[peer], "tm", peer).wait()
    high, low, _ = merge_shares(z_recv_l[...])
    factor = jnp.dot(high, expansion, preferred_element_type=F32)
    factor += jnp.dot(low, expansion, preferred_element_type=F32)
    piece = jnp.sum(
        factor.reshape(n_tm, piece_rows, width) * z_recv_u[...].astype(F32), axis=0
    )
    read_out[mine] = piece.astype(BF16)
    if pieces > 1:
        for peer in tm_peers:
            copy(
                read_out.at[my_tm], read_out.at[my_tm],
                ro_send.at[peer], ro_recv.at[my_tm], "tm", peer,
            ).start()
        for peer in tm_peers:
            copy(read_out.at[my_tm], read_out.at[peer], ro_send.at[peer], ro_recv.at[peer], "tm", peer).wait()

    own = pl.ds(pl.multiple_of(my_space * rows, rows), rows)
    merged[...] = latents_ref[own, :].astype(F32) + read_out[...].astype(F32).reshape(rows, width)
    normed = layer_norm(merged[...]).astype(BF16)
    up_copy.wait()
    hidden = jnp.dot(normed, up_ref[...], preferred_element_type=F32)
    hidden = (0.5 * hidden * (1.0 + lax.erf(hidden * (0.5 ** 0.5)))).astype(BF16)
    down_copy.wait()
    terms = jnp.dot(hidden, down_ref[...], preferred_element_type=F32)
    mlp_send[...] = terms.reshape(pieces, piece_rows, width).astype(BF16)
    for peer in tm_peers:
        copy(
            mlp_send.at[slot(peer)], mlp_recv.at[my_tm],
            mlp_ssem.at[peer], mlp_rsem.at[my_tm], "tm", peer,
        ).start()
    mlp_recv[my_tm] = mlp_send[mine]
    own_piece = pl.ds(pl.multiple_of(mine * piece_rows, piece_rows), piece_rows)
    for peer in tm_peers:
        copy(mlp_send.at[slot(peer)], mlp_recv.at[peer], mlp_ssem.at[peer], mlp_rsem.at[peer], "tm", peer).wait()
    all_latents[my_space, mine] = (
        merged[own_piece, :] + jnp.sum(mlp_recv[...].astype(F32), axis=0)
    ).astype(BF16)

    def piece_copy(space, part, peer, send_sem, recv_sem, axis="space"):
        block = all_latents.at[space, part]
        return copy(block, block, send_sem, recv_sem, axis, peer)

    def norm_block(space):
        block = all_latents[space].astype(F32).reshape(rows, width)
        write_values[space] = layer_norm(block).astype(BF16)

    def spread(part):
        for peer in far_peers:
            piece_copy(
                my_space, part, peer, gs_send.at[peer, part], gs_recv.at[my_space, part]
            ).start()
        pass_on(my_space, part)

    def pass_on(space, part):
        for peer in near_peers:
            piece_copy(
                space, part, peer, gn_send.at[space, part], gs_recv.at[space, part]
            ).start()

    if pieces > 1:
        for peer in tm_peers:
            piece_copy(
                my_space, my_tm, peer, gz_send.at[peer], gz_recv.at[my_tm], "tm"
            ).start()
    spread(mine)
    parts = [mine]
    if pieces > 1:
        for peer in tm_peers:
            piece_copy(
                my_space, peer, peer, gz_send.at[peer], gz_recv.at[peer], "tm"
            ).wait_recv()
            spread(peer)
            parts.append(peer)
    new_latents_ref[...] = (
        all_latents[my_space].astype(F32).reshape(rows, width).astype(BF16)
    )
    norm_block(my_space)
    for part in parts:
        for peer in far_peers:
            piece_copy(
                peer, part, peer, gs_send.at[peer, part], gs_recv.at[peer, part]
            ).wait_recv()
            pass_on(peer, part)
    for peer in far_peers:
        norm_block(peer)
    for part in parts:
        for near in near_peers:
            for space in [near] + [lax.rem(near + step, n_space) for step in far_steps]:
                piece_copy(
                    space, part, near, gn_send.at[my_space, part], gs_recv.at[space, part]
                ).wait_recv()
            for space in [my_space] + far_peers:
                piece_copy(
                    space, part, near, gn_send.at[space, part], gs_recv.at[space, part]
                ).wait_send()
        for peer in far_peers:
            piece_copy(
                my_space, part, peer, gs_send.at[peer, part], gs_recv.at[peer, part]
            ).wait_send()
    if pieces > 1:
        for peer in tm_peers:
            piece_copy(
                my_space, my_tm, peer, gz_send.at[peer], gz_recv.at[peer], "tm"
            ).wait_send()

    for near in near_peers:
        for space in [near] + [lax.rem(near + step, n_space) for step in far_steps]:
            norm_block(space)

    def write_pair(i, carry):
        lanes = pl.ds(pl.multiple_of(i * LANES, LANES), LANES)
        latent_pair = all_latents[:, :, :, lanes].astype(F32).reshape(latent_count, LANES)
        value_pair = write_values[:, :, lanes].astype(F32).reshape(latent_count, LANES)
        low = low_half(latent_count)
        key_parts = (
            jnp.where(low, latent_pair, 0.0).astype(BF16),
            jnp.where(low, 0.0, latent_pair).astype(BF16),
        )
        value_parts = (
            jnp.where(low, value_pair, 1.0).astype(BF16),
            jnp.where(low, 1.0, value_pair).astype(BF16),
        )
        share, _, _ = attend(keys_ref[:, lanes], key_parts, value_parts)
        new_tokens_ref[:, lanes] = (tokens_ref[:, lanes].astype(F32) + share).astype(BF16)
        return carry

    lax.fori_loop(0, pairs, write_pair, 0, unroll=4)


def on_device(n_tm, n_space, tokens, latents, up_weight, down_weight):
    token_count, width = tokens.shape
    latent_count = latents.shape[0]
    rows = latent_count // n_space
    pieces = n_tm if rows % (16 * n_tm) == 0 else 1
    piece_rows = rows // pieces
    pairs = width // LANES
    vmem = pl.BlockSpec(memory_space=pltpu.VMEM)
    anywhere = pl.BlockSpec(memory_space=pl.ANY)
    dma = pltpu.SemaphoreType.DMA
    scratch = [
        pltpu.VMEM(up_weight.shape, BF16),
        pltpu.VMEM(down_weight.shape, BF16),
        pltpu.VMEM((token_count, width), BF16),
        pltpu.VMEM((n_space // 2, pairs // 2, 2 * rows, LANES), BF16),
        pltpu.VMEM((n_space // 2, pairs // 2, 2 * rows, LANES), BF16),
        pltpu.VMEM((n_space // 2, 2 * rows, LANES), BF16),
        pltpu.VMEM((n_space // 2, 2 * rows, LANES), BF16),
        pltpu.VMEM((rows, width), F32),
        pltpu.VMEM((2, token_count, width // 2), BF16),
        pltpu.VMEM((2, token_count, width // 2), BF16),
        pltpu.VMEM((2, rows, width // 2), BF16),
        pltpu.VMEM((2, rows, LANES), F32),
        pltpu.VMEM((2, rows, width // 2), BF16),
        pltpu.VMEM((2, rows, LANES), F32),
        pltpu.VMEM((pieces, piece_rows, width), BF16),
        pltpu.VMEM((n_tm, piece_rows, width), BF16),
        pltpu.VMEM((pieces, piece_rows, LANES), F32),
        pltpu.VMEM((n_tm, piece_rows, LANES), F32),
        pltpu.VMEM((pieces, piece_rows, width), BF16),
        pltpu.VMEM((pieces, piece_rows, width), BF16),
        pltpu.VMEM((n_tm, piece_rows, width), BF16),
        pltpu.VMEM((n_space, pieces, piece_rows, width), BF16),
        pltpu.VMEM((n_space, rows, width), BF16),
        dma((2,)),
        dma((n_space,)), dma((n_space,)), dma((n_space,)), dma((n_space,)),
        dma((n_tm,)), dma((n_tm,)), dma((n_tm,)), dma((n_tm,)),
        dma((n_tm,)), dma((n_tm,)), dma((n_tm,)), dma((n_tm,)),
        dma((n_tm,)), dma((n_tm,)),
        dma((n_space, pieces)), dma((n_space, pieces)), dma((n_space, pieces)),
        dma((2,)), dma((2,)), dma((2,)), dma((2,)),
    ]
    return pl.pallas_call(
        functools.partial(kernel, n_tm, n_space, pieces),
        out_shape=(
            jax.ShapeDtypeStruct((token_count, width), BF16),
            jax.ShapeDtypeStruct((rows, width), BF16),
        ),
        in_specs=[vmem, vmem, anywhere, anywhere],
        out_specs=(vmem, vmem),
        scratch_shapes=scratch,
        compiler_params=pltpu.CompilerParams(
            collective_id=0, has_side_effects=True, vmem_limit_bytes=56 * 1024 * 1024
        ),
    )(tokens, latents, up_weight, down_weight)


def solution(mesh):
    n_tm, n_space = mesh.shape["tm"], mesh.shape["space"]
    in_specs = (P(("tm", "space"), None), P(), P(None, "tm"), P("tm", None))
    out_specs = (P(("tm", "space"), None), P("space", None))
    return jax.shard_map(
        functools.partial(on_device, n_tm, n_space),
        mesh=mesh, in_specs=in_specs, out_specs=out_specs, check_vma=False,
    )
```

```python
import functools

import jax
import jax.numpy as jnp
from jax import lax
from jax.experimental import pallas as pl
from jax.experimental.pallas import tpu as pltpu
from jax.sharding import PartitionSpec as P

H = 16
EPSILON = 1e-05
LANES = 128
MESH = pl.DeviceIdType.MESH
F32 = jnp.float32
BF16 = jnp.bfloat16


def layer_norm(values):
    center = values - jnp.mean(values, axis=-1, keepdims=True)
    spread = jnp.mean(center * center, axis=-1, keepdims=True)
    return center * lax.rsqrt(spread + EPSILON)


def dot_nt(left, right):
    return lax.dot_general(
        left, right, (((1,), (1,)), ((), ())), preferred_element_type=F32
    )


def low_half(rows):
    return lax.broadcasted_iota(jnp.int32, (rows, LANES), 1) < LANES // 2


def head_parts(pair, fill):
    values = pair.astype(F32)
    low = low_half(pair.shape[0])
    return (
        jnp.where(low, values, fill).astype(BF16),
        jnp.where(low, fill, values).astype(BF16),
    )


def attend(queries, key_parts, value_parts):
    results, peaks = [], []
    for keys, values in zip(key_parts, value_parts):
        scores = dot_nt(queries, keys)
        peak = jnp.max(scores, axis=-1, keepdims=True)
        weights = jnp.exp(scores - peak).astype(BF16)
        results.append(jnp.dot(weights, values, preferred_element_type=F32))
        peaks.append(peak)
    low = low_half(queries.shape[0])
    weighted = jnp.where(low, results[0], results[1])
    total = pltpu.roll(jnp.where(low, results[1], results[0]), LANES // 2, 1)
    return weighted / total, jnp.where(low, peaks[0], peaks[1]), total


def pair_expansion(width):
    lane = lax.broadcasted_iota(jnp.int32, (LANES, width), 0)
    feature = lax.broadcasted_iota(jnp.int32, (LANES, width), 1)
    half = LANES // 2
    wanted = (feature % LANES) // half * half + feature // LANES
    return jnp.where(lane == wanted, 1.0, 0.0).astype(BF16)


def merge_shares(logs):
    sources, rows, _ = logs.shape
    peak = jnp.max(logs, axis=0)
    weights = jnp.exp(logs - peak[None])
    total = jnp.sum(weights, axis=0)
    shares = (weights / total[None]).reshape(sources * rows, LANES)
    high = shares.astype(BF16)
    low = (shares - high.astype(F32)).astype(BF16)
    return high, low, peak + jnp.log(total)


def kernel(
    n_tm, n_space, pieces,
    tokens_ref, latents_ref, up_hbm, down_hbm, new_tokens_ref, new_latents_ref,
    up_ref, down_ref, keys_ref, send_u, recv_u, send_l, recv_l, merged,
    pair_tokens, pair_keys, half_u, half_l, pair_u, pair_l,
    z_send_u, z_recv_u, z_send_l, z_recv_l, read_out, mlp_send, mlp_recv,
    all_latents, write_values,
    weight_sem, su_send, su_recv, sl_send, sl_recv, zu_send, zu_recv, zl_send, zl_recv,
    ro_send, ro_recv, mlp_ssem, mlp_rsem, gz_send, gz_recv, gs_send, gs_recv,
    gn_send, pt_send, pt_recv, sw_send, sw_recv,
):
    my_tm = lax.axis_index("tm")
    my_space = lax.axis_index("space")
    width = tokens_ref.shape[1]
    latent_count = latents_ref.shape[0]
    pairs = width // LANES
    rows = latent_count // n_space
    piece_rows = rows // pieces
    scale = (width // H) ** (-0.5)

    def around(count, mine):
        return [lax.rem(mine + k, count) for k in range(1, count)]

    tm_peers = around(n_tm, my_tm)
    near_peers = [my_space + 1 - 2 * lax.rem(my_space, 2)]
    far_steps = range(2, n_space, 2)
    far_peers = [lax.rem(my_space + step, n_space) for step in far_steps]

    def copy(src, dst, send_sem, recv_sem, axis, peer):
        return pltpu.make_async_remote_copy(
            src_ref=src, dst_ref=dst, send_sem=send_sem, recv_sem=recv_sem,
            device_id={axis: peer}, device_id_type=MESH,
        )

    barrier = pltpu.get_barrier_semaphore()
    for peer in near_peers + far_peers:
        pl.semaphore_signal(barrier, inc=1, device_id={"space": peer}, device_id_type=MESH)
    for peer in tm_peers:
        pl.semaphore_signal(barrier, inc=1, device_id={"tm": peer}, device_id_type=MESH)
    up_copy = pltpu.make_async_copy(up_hbm, up_ref, weight_sem.at[0])
    down_copy = pltpu.make_async_copy(down_hbm, down_ref, weight_sem.at[1])
    up_copy.start()
    down_copy.start()

    pl.semaphore_wait(barrier, len(near_peers) + len(far_peers) + n_tm - 1)

    near = near_peers[0]
    parity = lax.rem(my_space, 2)
    chip = my_space // 2
    token_count = tokens_ref.shape[0]
    half_width = width // 2
    half_pairs = pairs // 2
    own_half = pl.ds(pl.multiple_of(parity * half_width, half_width), half_width)
    near_half = pl.ds(pl.multiple_of((1 - parity) * half_width, half_width), half_width)
    token_copy = copy(
        tokens_ref.at[:, near_half], pair_tokens.at[1], pt_send.at[0], pt_recv.at[0], "space", near
    )
    key_copy = copy(
        keys_ref.at[:, near_half], pair_keys.at[1], pt_send.at[1], pt_recv.at[1], "space", near
    )
    token_copy.start()
    keys_ref[...] = (
        layer_norm(tokens_ref[...].astype(F32)).astype(BF16).astype(F32) * scale
    ).astype(BF16)
    key_copy.start()
    pair_tokens[0] = tokens_ref[:, own_half]
    pair_keys[0] = keys_ref[:, own_half]
    expansion = pair_expansion(width)
    lane = lax.broadcasted_iota(jnp.int32, (latent_count, LANES), 1) % (LANES // 2)
    token_copy.wait()
    key_copy.wait()

    def read_pair(i, logs):
        lanes = pl.ds(pl.multiple_of(i * LANES, LANES), LANES)
        all_lanes = pl.ds(pl.multiple_of(parity * half_width + i * LANES, LANES), LANES)
        share, peak, total = attend(
            latents_ref[:, all_lanes],
            head_parts(pair_keys[:, :, lanes].reshape(2 * token_count, LANES), 0.0),
            head_parts(pair_tokens[:, :, lanes].reshape(2 * token_count, LANES), 1.0),
        )
        send_u[:, i] = share.reshape(n_space // 2, 2 * rows, LANES).astype(BF16)
        for peer in far_peers:
            copy(
                send_u.at[peer // 2, i], recv_u.at[chip, i],
                su_send.at[peer], su_recv.at[my_space], "space", peer,
            ).start()
        return jnp.where(lane == i, peak + jnp.log(total), logs)

    logs = lax.fori_loop(0, half_pairs, read_pair, jnp.zeros((latent_count, LANES), F32))
    first = logs.astype(BF16).astype(F32)
    second = (logs - first).astype(BF16).astype(F32)
    third = logs - first - second
    terms = jnp.where(
        lane < 16, first, jnp.where(lane < 32, pltpu.roll(second, 16, 1), pltpu.roll(third, 32, 1))
    )
    send_l[...] = terms.reshape(n_space // 2, 2 * rows, LANES).astype(BF16)
    for peer in far_peers:
        copy(
            send_l.at[peer // 2], recv_l.at[chip],
            sl_send.at[peer], sl_recv.at[my_space], "space", peer,
        ).start()
    recv_u[chip] = send_u[chip]
    recv_l[chip] = send_l[chip]
    for peer in far_peers:
        copy(send_l.at[peer // 2], recv_l.at[peer // 2], sl_send.at[peer], sl_recv.at[peer], "space", peer).wait()
    terms = recv_l[...].astype(F32).reshape(latent_count, LANES)
    logs = terms + pltpu.roll(terms, LANES - 16, 1) + pltpu.roll(terms, LANES - 32, 1)
    high, low, merged_log = merge_shares(logs.reshape(n_space // 2, 2 * rows, LANES))
    half_l[...] = merged_log.reshape(2, rows, LANES)
    for peer in far_peers:
        copy(send_u.at[peer // 2], recv_u.at[peer // 2], su_send.at[peer], su_recv.at[peer], "space", peer).wait()
    for i in range(half_pairs):
        lanes = slice(i * LANES, (i + 1) * LANES)
        factor = jnp.dot(high, expansion[:, lanes], preferred_element_type=F32)
        factor += jnp.dot(low, expansion[:, lanes], preferred_element_type=F32)
        half_u[:, :, lanes] = jnp.sum(
            factor.reshape(n_space // 2, 2 * rows, LANES) * recv_u[:, i].astype(F32), axis=0
        ).reshape(2, rows, LANES).astype(BF16)

    mine = my_tm if pieces > 1 else 0

    def slot(peer):
        return peer if pieces > 1 else 0

    def send_half(half, lanes):
        block = pair_u[half].astype(F32).reshape(pieces, piece_rows, half_width)
        z_send_u[:, :, lanes] = block.astype(BF16)
        for peer in tm_peers:
            copy(
                z_send_u.at[slot(peer), :, lanes], z_recv_u.at[my_tm, :, lanes],
                zu_send.at[peer], zu_recv.at[my_tm], "tm", peer,
            ).start()

    swap_l = copy(
        half_l.at[1 - parity], pair_l.at[parity], sw_send.at[0], sw_recv.at[0], "space", near
    )
    swap_u = copy(
        half_u.at[1 - parity], pair_u.at[parity], sw_send.at[1], sw_recv.at[1], "space", near
    )
    swap_l.start()
    swap_u.start()
    pair_l[parity] = half_l[parity]
    pair_u[parity] = half_u[parity]
    send_half(parity, own_half)
    copy(half_l.at[1 - parity], pair_l.at[1 - parity], sw_send.at[0], sw_recv.at[0], "space", near).wait()
    copy(half_u.at[1 - parity], pair_u.at[1 - parity], sw_send.at[1], sw_recv.at[1], "space", near).wait()
    row_lane = lax.broadcasted_iota(jnp.int32, (rows, LANES), 1) % (LANES // 2)
    merged_log = jnp.where(row_lane < half_pairs, pair_l[0], pltpu.roll(pair_l[1], half_pairs, 1))

    z_send_l[...] = merged_log.reshape(pieces, piece_rows, LANES)
    for peer in tm_peers:
        copy(
            z_send_l.at[slot(peer)], z_recv_l.at[my_tm],
            zl_send.at[peer], zl_recv.at[my_tm], "tm", peer,
        ).start()
    send_half(1 - parity, near_half)
    z_recv_u[my_tm] = z_send_u[mine]
    z_recv_l[my_tm] = z_send_l[mine]
    for peer in tm_peers:
        copy(z_send_l.at[slot(peer)], z_recv_l.at[peer], zl_send.at[peer], zl_recv.at[peer], "tm", peer).wait()
        copy(z_send_u.at[slot(peer)], z_recv_u.at[peer], zu_send.at[peer], zu_recv.at[peer], "tm", peer).wait()
    high, low, _ = merge_shares(z_recv_l[...])
    factor = jnp.dot(high, expansion, preferred_element_type=F32)
    factor += jnp.dot(low, expansion, preferred_element_type=F32)
    piece = jnp.sum(
        factor.reshape(n_tm, piece_rows, width) * z_recv_u[...].astype(F32), axis=0
    )
    read_out[mine] = piece.astype(BF16)
    if pieces > 1:
        for peer in tm_peers:
            copy(
                read_out.at[my_tm], read_out.at[my_tm],
                ro_send.at[peer], ro_recv.at[my_tm], "tm", peer,
            ).start()
        for peer in tm_peers:
            copy(read_out.at[my_tm], read_out.at[peer], ro_send.at[peer], ro_recv.at[peer], "tm", peer).wait()

    own = pl.ds(pl.multiple_of(my_space * rows, rows), rows)
    merged[...] = latents_ref[own, :].astype(F32) + read_out[...].astype(F32).reshape(rows, width)
    normed = layer_norm(merged[...]).astype(BF16)
    up_copy.wait()
    hidden = jnp.dot(normed, up_ref[...], preferred_element_type=F32)
    hidden = (0.5 * hidden * (1.0 + lax.erf(hidden * (0.5 ** 0.5)))).astype(BF16)
    down_copy.wait()
    terms = jnp.dot(hidden, down_ref[...], preferred_element_type=F32)
    mlp_send[...] = terms.reshape(pieces, piece_rows, width).astype(BF16)
    for peer in tm_peers:
        copy(
            mlp_send.at[slot(peer)], mlp_recv.at[my_tm],
            mlp_ssem.at[peer], mlp_rsem.at[my_tm], "tm", peer,
        ).start()
    mlp_recv[my_tm] = mlp_send[mine]
    own_piece = pl.ds(pl.multiple_of(mine * piece_rows, piece_rows), piece_rows)
    for peer in tm_peers:
        copy(mlp_send.at[slot(peer)], mlp_recv.at[peer], mlp_ssem.at[peer], mlp_rsem.at[peer], "tm", peer).wait()
    all_latents[my_space, mine] = (
        merged[own_piece, :] + jnp.sum(mlp_recv[...].astype(F32), axis=0)
    ).astype(BF16)

    def piece_copy(space, part, peer, send_sem, recv_sem, axis="space"):
        block = all_latents.at[space, part]
        return copy(block, block, send_sem, recv_sem, axis, peer)

    def norm_block(space):
        block = all_latents[space].astype(F32).reshape(rows, width)
        write_values[space] = layer_norm(block).astype(BF16)

    def spread(part):
        for peer in far_peers:
            piece_copy(
                my_space, part, peer, gs_send.at[peer, part], gs_recv.at[my_space, part]
            ).start()
        pass_on(my_space, part)

    def pass_on(space, part):
        for peer in near_peers:
            piece_copy(
                space, part, peer, gn_send.at[space, part], gs_recv.at[space, part]
            ).start()

    if pieces > 1:
        for peer in tm_peers:
            piece_copy(
                my_space, my_tm, peer, gz_send.at[peer], gz_recv.at[my_tm], "tm"
            ).start()
    spread(mine)
    parts = [mine]
    if pieces > 1:
        for peer in tm_peers:
            piece_copy(
                my_space, peer, peer, gz_send.at[peer], gz_recv.at[peer], "tm"
            ).wait_recv()
            spread(peer)
            parts.append(peer)
    new_latents_ref[...] = (
        all_latents[my_space].astype(F32).reshape(rows, width).astype(BF16)
    )
    norm_block(my_space)
    for part in parts:
        for peer in far_peers:
            piece_copy(
                peer, part, peer, gs_send.at[peer, part], gs_recv.at[peer, part]
            ).wait_recv()
            pass_on(peer, part)
    for peer in far_peers:
        norm_block(peer)
    for part in parts:
        for near in near_peers:
            for space in [near] + [lax.rem(near + step, n_space) for step in far_steps]:
                piece_copy(
                    space, part, near, gn_send.at[my_space, part], gs_recv.at[space, part]
                ).wait_recv()
            for space in [my_space] + far_peers:
                piece_copy(
                    space, part, near, gn_send.at[space, part], gs_recv.at[space, part]
                ).wait_send()
        for peer in far_peers:
            piece_copy(
                my_space, part, peer, gs_send.at[peer, part], gs_recv.at[peer, part]
            ).wait_send()
    if pieces > 1:
        for peer in tm_peers:
            piece_copy(
                my_space, my_tm, peer, gz_send.at[peer], gz_recv.at[peer], "tm"
            ).wait_send()

    for near in near_peers:
        for space in [near] + [lax.rem(near + step, n_space) for step in far_steps]:
            norm_block(space)

    def write_pair(i, carry):
        lanes = pl.ds(pl.multiple_of(i * LANES, LANES), LANES)
        latent_pair = all_latents[:, :, :, lanes].astype(F32).reshape(latent_count, LANES)
        value_pair = write_values[:, :, lanes].astype(F32).reshape(latent_count, LANES)
        low = low_half(latent_count)
        key_parts = (
            jnp.where(low, latent_pair, 0.0).astype(BF16),
            jnp.where(low, 0.0, latent_pair).astype(BF16),
        )
        value_parts = (
            jnp.where(low, value_pair, 1.0).astype(BF16),
            jnp.where(low, 1.0, value_pair).astype(BF16),
        )
        share, _, _ = attend(keys_ref[:, lanes], key_parts, value_parts)
        new_tokens_ref[:, lanes] = (tokens_ref[:, lanes].astype(F32) + share).astype(BF16)
        return carry

    lax.fori_loop(0, pairs, write_pair, 0, unroll=4)


def on_device(n_tm, n_space, tokens, latents, up_weight, down_weight):
    token_count, width = tokens.shape
    latent_count = latents.shape[0]
    rows = latent_count // n_space
    pieces = n_tm if rows % (16 * n_tm) == 0 else 1
    piece_rows = rows // pieces
    pairs = width // LANES
    vmem = pl.BlockSpec(memory_space=pltpu.VMEM)
    anywhere = pl.BlockSpec(memory_space=pl.ANY)
    dma = pltpu.SemaphoreType.DMA
    scratch = [
        pltpu.VMEM(up_weight.shape, BF16),
        pltpu.VMEM(down_weight.shape, BF16),
        pltpu.VMEM((token_count, width), BF16),
        pltpu.VMEM((n_space // 2, pairs // 2, 2 * rows, LANES), BF16),
        pltpu.VMEM((n_space // 2, pairs // 2, 2 * rows, LANES), BF16),
        pltpu.VMEM((n_space // 2, 2 * rows, LANES), BF16),
        pltpu.VMEM((n_space // 2, 2 * rows, LANES), BF16),
        pltpu.VMEM((rows, width), F32),
        pltpu.VMEM((2, token_count, width // 2), BF16),
        pltpu.VMEM((2, token_count, width // 2), BF16),
        pltpu.VMEM((2, rows, width // 2), BF16),
        pltpu.VMEM((2, rows, LANES), F32),
        pltpu.VMEM((2, rows, width // 2), BF16),
        pltpu.VMEM((2, rows, LANES), F32),
        pltpu.VMEM((pieces, piece_rows, width), BF16),
        pltpu.VMEM((n_tm, piece_rows, width), BF16),
        pltpu.VMEM((pieces, piece_rows, LANES), F32),
        pltpu.VMEM((n_tm, piece_rows, LANES), F32),
        pltpu.VMEM((pieces, piece_rows, width), BF16),
        pltpu.VMEM((pieces, piece_rows, width), BF16),
        pltpu.VMEM((n_tm, piece_rows, width), BF16),
        pltpu.VMEM((n_space, pieces, piece_rows, width), BF16),
        pltpu.VMEM((n_space, rows, width), BF16),
        dma((2,)),
        dma((n_space,)), dma((n_space,)), dma((n_space,)), dma((n_space,)),
        dma((n_tm,)), dma((n_tm,)), dma((n_tm,)), dma((n_tm,)),
        dma((n_tm,)), dma((n_tm,)), dma((n_tm,)), dma((n_tm,)),
        dma((n_tm,)), dma((n_tm,)),
        dma((n_space, pieces)), dma((n_space, pieces)), dma((n_space, pieces)),
        dma((2,)), dma((2,)), dma((2,)), dma((2,)),
    ]
    return pl.pallas_call(
        functools.partial(kernel, n_tm, n_space, pieces),
        out_shape=(
            jax.ShapeDtypeStruct((token_count, width), BF16),
            jax.ShapeDtypeStruct((rows, width), BF16),
        ),
        in_specs=[vmem, vmem, anywhere, anywhere],
        out_specs=(vmem, vmem),
        scratch_shapes=scratch,
        compiler_params=pltpu.CompilerParams(
            collective_id=0, has_side_effects=True, vmem_limit_bytes=56 * 1024 * 1024
        ),
    )(tokens, latents, up_weight, down_weight)


def solution(mesh):
    n_tm, n_space = mesh.shape["tm"], mesh.shape["space"]
    in_specs = (P(("tm", "space"), None), P(), P(None, "tm"), P("tm", None))
    out_specs = (P(("tm", "space"), None), P("space", None))
    return jax.shard_map(
        functools.partial(on_device, n_tm, n_space),
        mesh=mesh, in_specs=in_specs, out_specs=out_specs, check_vma=False,
    )
```
